512 devices in a mesh: dp: 4 (over y_hi), expert: 32 (over z, y_lo, core), context: 4 (over x).
Axes of the slice: x: 4, y: 8 (y_hi: 4, y_lo: 2; y = y_hi * 2 + y_lo), z: 8, core: 2. Of those that a mesh axis runs over, the one named last changes fastest.
Arguments:
- grad_out: bfloat16 [65536, 4096], P(('dp', 'expert', 'context')), may hold values from -6 to 6
- routes: int32 [65536, 8], P(('dp', 'expert', 'context')), may hold values from 0 to 127, all different within a row; in each aligned block of 128 rows (0 to 127, 128 to 255, ...) at most 16 rows name the same one
- route_weight: bfloat16 [65536, 8], P(('dp', 'expert', 'context')), may hold values from 0.099609375 to 1
- saved_gate: bfloat16 [4, 32, 4, 32, 16, 768], P('dp', 'expert', 'context'), may hold values from -6 to 6
- saved_up: bfloat16 [4, 32, 4, 32, 16, 768], P('dp', 'expert', 'context'), may hold values from -6 to 6
- down_weight: bfloat16 [32, 768, 4096], P('expert', None, ('dp', 'context')), may hold values from -0.21875 to 0.21875
Outputs:
- grad_gate: bfloat16 [4, 32, 4, 32, 16, 768], P('dp', 'expert', 'context')
- grad_up: bfloat16 [4, 32, 4, 32, 16, 768], P('dp', 'expert', 'context')
- grad_weight: float32 [65536, 8], P(('dp', 'expert', 'context'))
The draws below stay inside these ranges and needn't reach their ends.
Inputs may be any that keep to these rules, and one draw needn't show every extreme that they name: `routes`: each row names 8 different experts; among the rows of one device no expert is named by more than 16 rows.
All inputs are finite; a program needn't handle non-finite values.
Results may differ from the reference program's by a relative error of at most 0.003.
Values may be sent and summed in bfloat16 or wider, within the bound.
No kernel may reach another device: no remote copies, remote signals or barrier semaphores. Data moves between devices by JAX's collectives and lax.ppermute only.
A program may use at most 64 MiB of HBM per device.

```python
import math
import jax
import jax.numpy as jnp
import numpy as np
from jax import lax

D = 4096
EXPERTS = 128
TOPK = 8
H = 768
TOK_DEV = 128
CAP = 16
TOKENS = 65536
N_DP = 4
N_EXPERT = 32
N_CONTEXT = 4


def block_scale(own_key, shape, cuts, low, largest):
    loudness = 1.0
    for axis_at, blocks in cuts:
        draws = jax.random.uniform(jax.random.fold_in(jax.random.fold_in(own_key, 6), axis_at), (blocks,), jnp.float32, low / len(cuts), largest / len(cuts))
        loudness = loudness * jnp.repeat(jnp.exp(draws), shape[axis_at] // blocks).reshape((-1,) + (1,) * (len(shape) - 1 - axis_at))
    return loudness


def deal_out(rng, own, number, rows, amount, top, bound, slope):
    ranking = jax.random.permutation(rng, amount)
    crowded, ordinary = shares(amount, rows * top, bound, slope, True), shares(amount, rows * top, bound, slope, False)
    places = jnp.arange(amount)

    def named(sizes, turn):
        used = int((sizes > 0).sum())
        fixed = max(1, used // 4)
        moved = fixed + (places - fixed + turn * (used - fixed)) % max(1, amount - fixed)
        return jnp.zeros((amount,), jnp.int32).at[ranking[jnp.where(places < fixed, places, moved)]].set(jnp.asarray(sizes, jnp.int32))

    sizes = jnp.where(number % 4 == 0, named(crowded, number // 4), named(ordinary, number - number // 4 - 1))
    mixed = jax.random.permutation(jax.random.fold_in(own, 3), amount)
    donor, receiver = mixed[0:amount // 2 * 2:2], mixed[1:amount // 2 * 2:2]
    room = jnp.minimum(sizes[donor] - 1, bound - sizes[receiver]) // 2
    room = jnp.where((donor == ranking[0]) | (receiver == ranking[0]) | (sizes[receiver] == 0), 0, jnp.maximum(room, 0))
    moved = jax.random.randint(jax.random.fold_in(own, 4), (amount // 2,), 0, 1 << 20) % (room + 1)
    sizes = sizes.at[donor].add(-moved).at[receiver].add(moved)
    members = jnp.searchsorted(jnp.cumsum(sizes), jnp.arange(rows * top), side="right").astype(jnp.int32)
    grid = members.reshape(top, rows).T
    grid = grid[jax.random.permutation(jax.random.fold_in(own, 1), rows)]
    turn = jax.random.randint(jax.random.fold_in(own, 2), (rows, 1), 0, top)
    return jnp.take_along_axis(grid, (jnp.arange(top)[None, :] + turn) % top, axis=1)


def shares(number_of, total, reach, skew, full):
    loads = [(1 << 20) // math.isqrt(standing ** skew) + 1 for standing in range(1, number_of + 1)]
    largest = reach if full else min(reach, max(-(-total // number_of), total * loads[0] // sum(loads)))
    least = 1 if total - largest >= number_of - 1 else 0
    holding, surplus = [largest] + [least] * (number_of - 1), total - largest - least * (number_of - 1)
    while surplus > 0:
        candidates = [i for i in range(1, number_of) if holding[i] < largest] or [i for i in range(1, number_of) if holding[i] < reach]
        mass, budget = sum([loads[i] for i in candidates]), surplus
        for i in candidates:
            extra = min(reach - holding[i], max(1, budget * loads[i] // mass), surplus)
            holding[i] = holding[i] + extra
            surplus = surplus - extra
    return np.array(holding)


def noise(rng, shape, deviation, limit, pieces=(), held_as=jnp.bfloat16):
    factor_of = block_scale(rng, shape, pieces, -0.22, 0.18) if pieces else 1.0
    values = jax.random.normal(rng, shape, jnp.float32) * deviation * factor_of
    return jnp.minimum(jnp.maximum(values, -limit), limit).astype(held_as)


def setup_inputs(seed: int = 0) -> dict:
    keys = jax.random.split(jax.random.key(seed), 7)
    grad_out = noise(keys[0], (TOKENS, D), 0.5, 6.0, ((0, 512),))
    routes_keys = jax.random.split(jax.random.fold_in(keys[1], 1), TOKENS // TOK_DEV)
    routes_turns = jax.random.permutation(jax.random.fold_in(keys[1], 3), TOKENS // TOK_DEV)
    routes = jax.vmap(lambda own, number: deal_out(jax.random.fold_in(keys[1], 2), own, number, TOK_DEV, EXPERTS, TOPK, CAP, 2))(routes_keys, routes_turns).reshape((TOKENS, TOPK))
    route_weight = jnp.clip(jnp.exp(math.log(1.0) - 2.306499 * jax.random.uniform(keys[2], (TOKENS, TOPK), jnp.float32) ** block_scale(keys[2], (TOKENS, TOPK), ((0, 512),), -0.2, 0.2)), 0.099609375, 1.0).astype(jnp.bfloat16)
    saved_gate = noise(keys[3], (N_DP, N_EXPERT, N_CONTEXT, N_EXPERT, CAP, H), 1.0, 6.0, ((0, 4), (1, 32), (2, 4)))
    saved_up = noise(keys[4], (N_DP, N_EXPERT, N_CONTEXT, N_EXPERT, CAP, H), 1.0, 6.0, ((0, 4), (1, 32), (2, 4)))
    down_weight = noise(keys[5], (N_EXPERT, H, D), H ** -0.5, 0.21875, ((0, 32), (2, 16)))
    return dict(grad_out=grad_out, routes=routes, route_weight=route_weight, saved_gate=saved_gate, saved_up=saved_up, down_weight=down_weight)


def slot_positions(routes_dev, ranks, cap, per_rank):
    flat = routes_dev.reshape(-1)
    served = jnp.arange(ranks, dtype=jnp.int32) * per_rank
    hits = (flat[:, None] == served[None, :]).astype(jnp.int32)
    before = jnp.cumsum(hits, axis=0) - hits
    target = before + (jnp.arange(ranks, dtype=jnp.int32) * cap)[None, :]
    live = jnp.sum(hits, axis=1) > 0
    return jnp.where(live, jnp.sum(hits * target, axis=1), -1).astype(jnp.int32)


def expert_math(back, slot_weight, gate, up):
    gate_f = gate.astype(jnp.float32)
    up_f = up.astype(jnp.float32)
    sigma = jax.nn.sigmoid(gate_f)
    hidden = (gate_f * sigma * up_f).astype(jnp.bfloat16)
    hidden = lax.optimization_barrier(hidden)
    slot_grad = jnp.sum(hidden.astype(jnp.float32) * back, axis=-1)
    grad_hidden = slot_weight.astype(jnp.float32)[..., None] * back
    grad_gate = (grad_hidden * up_f * sigma * (1.0 + gate_f * (1.0 - sigma))).astype(jnp.bfloat16)
    grad_up = (grad_hidden * gate_f * sigma).astype(jnp.bfloat16)
    return grad_gate, grad_up, slot_grad


def reference(grad_out, routes, route_weight, saved_gate, saved_up, down_weight):
    ranks = N_EXPERT
    slots = ranks * CAP
    per_rank = EXPERTS // ranks

    def group_view(array):
        last = array.shape[1]
        shaped = array.reshape(N_DP, ranks, N_CONTEXT, TOK_DEV, last).transpose(0, 2, 1, 3, 4)
        return shaped.reshape(N_DP * N_CONTEXT, ranks, TOK_DEV, last)

    def saved_view(array):
        return array.transpose(0, 2, 1, 3, 4, 5).reshape(N_DP * N_CONTEXT, ranks, ranks, CAP, H)

    def one_group(items):
        outs_s, routes_s, weights_s, gate_r, up_r = items

        def one_source(source):
            dout, route_rows, weight_rows = source
            position = slot_positions(route_rows, ranks, CAP, per_rank)
            onehot = position[:, None] == jnp.arange(slots, dtype=jnp.int32)[None, :]
            choose = onehot.reshape(TOK_DEV, TOPK, slots).any(axis=1).astype(jnp.bfloat16)
            sent = jnp.dot(choose.T, dout, preferred_element_type=jnp.float32).astype(jnp.bfloat16)
            weights = jnp.sum(jnp.where(onehot, weight_rows.reshape(-1)[:, None].astype(jnp.float32), 0.0), axis=0)
            return sent.reshape(ranks, CAP, D), weights.astype(jnp.bfloat16).reshape(ranks, CAP), onehot

        sent, slot_weight, onehots = lax.map(one_source, (outs_s, routes_s, weights_s))

        def one_expert(expert_items):
            received, received_weight, weight, gate, up = expert_items
            back = jnp.dot(received.reshape(-1, D), weight.T, preferred_element_type=jnp.float32)
            return expert_math(back.reshape(ranks, CAP, H), received_weight, gate, up)

        grad_gate, grad_up, slot_grad = lax.map(
            one_expert, (sent.transpose(1, 0, 2, 3), slot_weight.transpose(1, 0, 2), down_weight, gate_r, up_r))
        returned = slot_grad.transpose(1, 0, 2).reshape(ranks, slots)
        grad_weight = jnp.sum(jnp.where(onehots, returned[:, None, :], 0.0), axis=-1)
        return grad_gate, grad_up, grad_weight.reshape(ranks, TOK_DEV, TOPK)

    grad_gate, grad_up, grad_weight = lax.map(
        one_group, (group_view(grad_out), group_view(routes), group_view(route_weight),
                    saved_view(saved_gate), saved_view(saved_up)))

    def unview(array):
        return array.reshape(N_DP, N_CONTEXT, ranks, ranks, CAP, H).transpose(0, 2, 1, 3, 4, 5)

    grad_weight = grad_weight.reshape(N_DP, N_CONTEXT, ranks, TOK_DEV, TOPK).transpose(0, 2, 1, 3, 4)
    return unview(grad_gate), unview(grad_up), grad_weight.reshape(TOKENS, TOPK)
```

```python
import jax
import jax.numpy as jnp
from jax import lax
from jax.experimental import pallas as pl
from jax.experimental.pallas import tpu as pltpu
from jax.sharding import PartitionSpec as P

EXPERTS = 128


def head_kernel(ranks, cap, n_dp, n_context, routes_ref, weight_ref, grad_ref, sent_ref, slot_weight_ref, slot_ref):
    topk, tokens = routes_ref.shape
    slots = ranks * cap
    step = EXPERTS // ranks
    served = lax.broadcasted_iota(jnp.int32, (ranks, tokens), 0) * step
    hits = jnp.zeros((ranks, tokens), jnp.float32)
    picked = jnp.zeros((ranks, tokens), jnp.float32)
    for k in range(topk):
        hit = routes_ref[k : k + 1, :] == served
        hits = hits + jnp.where(hit, 1.0, 0.0)
        picked = picked + jnp.where(hit, weight_ref[k : k + 1, :].astype(jnp.float32), 0.0)
    earlier = lax.broadcasted_iota(jnp.int32, (tokens, tokens), 0) < lax.broadcasted_iota(
        jnp.int32, (tokens, tokens), 1
    )
    earlier = jnp.where(earlier, 1.0, 0.0).astype(jnp.bfloat16)
    before = jnp.dot(hits.astype(jnp.bfloat16), earlier, preferred_element_type=jnp.float32)
    slot = jnp.where(hits > 0.0, before, -1.0)
    slot_ref[...] = slot
    lane = lax.broadcasted_iota(jnp.int32, (ranks, cap), 1).astype(jnp.float32)
    found = jnp.zeros((ranks, cap), jnp.float32)
    for j in range(cap):
        one = jnp.sum(jnp.where(slot == float(j), picked, 0.0), axis=1, keepdims=True)
        found = jnp.where(lane == float(j), one, found)
    slot_weight_ref[...] = found.astype(jnp.bfloat16)
    wide = jnp.broadcast_to(slot[:, None, :], (ranks, cap, tokens))
    place = lax.broadcasted_iota(jnp.int32, (ranks, cap, tokens), 1).astype(jnp.float32)
    choose = jnp.where(wide == place, 1.0, 0.0).reshape(slots, tokens).astype(jnp.bfloat16)
    a = lax.axis_index("dp")
    c = lax.axis_index("context")
    cols = grad_ref.shape[1] // (n_dp * n_context)
    for j in range(n_context):
        for i in range(n_dp):
            block = lax.rem(a + i, n_dp) * n_context + lax.rem(c + j, n_context)
            part = grad_ref[:, pl.ds(pl.multiple_of(block * cols, cols), cols)]
            out = jnp.dot(choose, part, preferred_element_type=jnp.float32).astype(jnp.bfloat16)
            at = (j * n_dp + i) * cols
            sent_ref[:, at : at + cols] = out


def head(routes, route_weight, grad_out, ranks, cap, n_dp, n_context):
    tokens, width = grad_out.shape

    def kernel(*refs):
        head_kernel(ranks, cap, n_dp, n_context, *refs)

    return pl.pallas_call(
        kernel,
        out_shape=(
            jax.ShapeDtypeStruct((ranks * cap, width), jnp.bfloat16),
            jax.ShapeDtypeStruct((ranks, cap), jnp.bfloat16),
            jax.ShapeDtypeStruct((ranks, tokens), jnp.float32),
        ),
        compiler_params=pltpu.CompilerParams(vmem_limit_bytes=32 * 2**20),
        name="head",
    )(routes.T, route_weight.T, grad_out)


def project_kernel(cap, received_ref, hidden_ref, *refs):
    *weights, back_ref, slot_grad_ref = refs
    rows, units = hidden_ref.shape
    total = jnp.zeros((rows, units), jnp.float32)
    at = 0
    for weight_ref in weights:
        for i in range(weight_ref.shape[0]):
            cols = weight_ref.shape[2]
            total = total + lax.dot_general(
                received_ref[:, at : at + cols],
                weight_ref[i],
                (((1,), (1,)), ((), ())),
                preferred_element_type=jnp.float32,
            )
            at += cols
    back_ref[...] = total
    grads = hidden_ref[...].astype(jnp.float32) * total
    slot_grad_ref[...] = jnp.sum(grads.reshape(rows // cap, cap, units), axis=2)


def project(received, hidden, weights, cap):
    rows, units = hidden.shape

    def kernel(*refs):
        project_kernel(cap, *refs)

    return pl.pallas_call(
        kernel,
        out_shape=(
            jax.ShapeDtypeStruct((rows, units), jnp.float32),
            jax.ShapeDtypeStruct((rows // cap, cap), jnp.float32),
        ),
        compiler_params=pltpu.CompilerParams(vmem_limit_bytes=32 * 2**20),
        name="project",
    )(received, hidden, *weights)


def tail_kernel(routes_ref, slot_ref, returned_ref, out_ref):
    ranks, cap = returned_ref.shape
    topk, tokens = routes_ref.shape
    slot = slot_ref[...]
    grads = jnp.zeros((ranks, tokens), jnp.float32)
    for j in range(cap):
        grads = grads + jnp.where(slot == float(j), returned_ref[:, j : j + 1], 0.0)
    served = lax.broadcasted_iota(jnp.int32, (ranks, tokens), 0) * (EXPERTS // ranks)
    for k in range(topk):
        hit = routes_ref[k : k + 1, :] == served
        out_ref[k : k + 1, :] = jnp.sum(jnp.where(hit, grads, 0.0), axis=0, keepdims=True)


def tail(routes, slot, returned):
    return pl.pallas_call(
        tail_kernel,
        out_shape=jax.ShapeDtypeStruct((routes.shape[1], routes.shape[0]), jnp.float32),
        compiler_params=pltpu.CompilerParams(vmem_limit_bytes=8 * 2**20),
        name="tail",
    )(routes.T, slot, returned).T


def ring_gather(block, axis):
    size = lax.axis_size(axis)
    up = [(i, (i + 1) % size) for i in range(size)]
    down = [(i, (i - 1) % size) for i in range(size)]
    half = block.shape[0] // 2
    before = lax.ppermute(block, axis, up)
    after = lax.ppermute(block, axis, down)
    far_low = lax.ppermute(before[:half], axis, up)
    far_high = lax.ppermute(after[half:], axis, down)
    return after, far_low, far_high, before


def body(grad_out, routes, route_weight, saved_gate, saved_up, down_weight):
    ranks = lax.axis_size("expert")
    n_dp, n_context = lax.axis_size("dp"), lax.axis_size("context")
    cap, units = saved_gate.shape[4:]
    slots = ranks * cap
    width = grad_out.shape[1]

    own = down_weight[0]
    after, far_low, far_high, before = ring_gather(own, "dp")
    over_dp = jnp.concatenate([own, after, far_low, far_high, before], axis=0)
    over_dp = over_dp.reshape(n_dp, units, own.shape[1])
    after, far_low, far_high, before = ring_gather(over_dp, "context")
    weights = (over_dp, after, far_low, far_high, before)

    sent, slot_weight, slot = head(routes, route_weight, grad_out, ranks, cap, n_dp, n_context)
    received = lax.all_to_all(
        sent.reshape(ranks, cap, width), "expert", split_axis=0, concat_axis=0, tiled=True
    ).reshape(slots, width)
    slot_weight = lax.all_to_all(slot_weight, "expert", split_axis=0, concat_axis=0, tiled=True)

    gate = saved_gate.reshape(slots, units).astype(jnp.float32)
    up = saved_up.reshape(slots, units).astype(jnp.float32)
    sigma = jax.nn.sigmoid(gate)
    hidden = lax.optimization_barrier((gate * sigma * up).astype(jnp.bfloat16))
    back, slot_grad = project(received, hidden, weights, cap)
    returned = lax.all_to_all(slot_grad, "expert", split_axis=0, concat_axis=0, tiled=True)
    grad_weight = tail(routes, slot, returned)

    grad_hidden = slot_weight.reshape(slots, 1).astype(jnp.float32) * back
    grad_gate = (grad_hidden * up * sigma * (1.0 + gate * (1.0 - sigma))).astype(jnp.bfloat16)
    grad_up = (grad_hidden * gate * sigma).astype(jnp.bfloat16)
    return grad_gate.reshape(saved_gate.shape), grad_up.reshape(saved_up.shape), grad_weight


def solution(mesh):
    tokens = P(("dp", "expert", "context"), None)
    saved = P("dp", "expert", "context", None, None, None)
    return jax.shard_map(
        body,
        mesh=mesh,
        in_specs=(tokens, tokens, tokens, saved, saved, P("expert", None, ("dp", "context"))),
        out_specs=(saved, saved, tokens),
        check_vma=False,
    )
```

```python
import jax
import jax.numpy as jnp
from jax import lax
from jax.experimental import pallas as pl
from jax.experimental.pallas import tpu as pltpu
from jax.sharding import PartitionSpec as P

EXPERTS = 128
VMEM = 60 * 2**20
HBM = pl.BlockSpec(memory_space=pltpu.HBM)


def served_experts(ranks, tokens):
    return lax.broadcasted_iota(jnp.int32, (ranks, tokens), 0) * (EXPERTS // ranks)


def head_kernel(ranks, cap, n_dp, n_context, routes_ref, weight_ref, grad_hbm, sent_hbm, slot_weight_ref, slot_ref, grad, sent, grad_sem, sent_sem):
    topk, tokens = routes_ref.shape
    slots = ranks * cap
    load = pltpu.make_async_copy(grad_hbm, grad, grad_sem)
    load.start()
    served = served_experts(ranks, tokens)
    hits = jnp.zeros((ranks, tokens), jnp.float32)
    picked = jnp.zeros((ranks, tokens), jnp.float32)
    for k in range(topk):
        hit = routes_ref[k : k + 1, :] == served
        hits = hits + jnp.where(hit, 1.0, 0.0)
        picked = picked + jnp.where(hit, weight_ref[k : k + 1, :].astype(jnp.float32), 0.0)
    earlier = lax.broadcasted_iota(jnp.int32, (tokens, tokens), 0) < lax.broadcasted_iota(
        jnp.int32, (tokens, tokens), 1
    )
    earlier = jnp.where(earlier, 1.0, 0.0).astype(jnp.bfloat16)
    before = jnp.dot(hits.astype(jnp.bfloat16), earlier, preferred_element_type=jnp.float32)
    slot = jnp.where(hits > 0.0, before, -1.0)
    slot_ref[...] = slot
    wide = jnp.broadcast_to(slot[:, None, :], (ranks, cap, tokens))
    place = lax.broadcasted_iota(jnp.int32, (ranks, cap, tokens), 1).astype(jnp.float32)
    choose = jnp.where(wide == place, 1.0, 0.0).reshape(slots, tokens).astype(jnp.bfloat16)
    load.wait()
    c = lax.axis_index("context")
    cols = grad.shape[1] // (n_dp * n_context)
    group = n_dp * cols
    stores = []
    for j in range(n_context):
        for i in range(n_dp):
            block = i * n_context + lax.rem(c + j, n_context)
            part = grad[:, pl.ds(pl.multiple_of(block * cols, cols), cols)]
            at = j * group + i * cols
            out = jnp.dot(choose, part, preferred_element_type=jnp.float32)
            sent[:, at : at + cols] = out.astype(jnp.bfloat16)
        where = pl.ds(j * group, group)
        store = pltpu.make_async_copy(sent.at[:, where], sent_hbm.at[:, where], sent_sem.at[j])
        store.start()
        stores.append(store)
    lane = lax.broadcasted_iota(jnp.int32, (ranks, cap), 1).astype(jnp.float32)
    found = jnp.zeros((ranks, cap), jnp.float32)
    for j in range(cap):
        one = jnp.sum(jnp.where(slot == float(j), picked, 0.0), axis=1, keepdims=True)
        found = jnp.where(lane == float(j), one, found)
    slot_weight_ref[...] = found
    for store in stores:
        store.wait()


def head(routes, route_weight, grad_out, ranks, cap, n_dp, n_context):
    tokens, width = grad_out.shape

    def kernel(*refs):
        head_kernel(ranks, cap, n_dp, n_context, *refs)

    whole = pl.BlockSpec(memory_space=pltpu.VMEM)
    return pl.pallas_call(
        kernel,
        out_shape=(
            jax.ShapeDtypeStruct((ranks * cap, width), jnp.bfloat16),
            jax.ShapeDtypeStruct((ranks, cap), jnp.float32),
            jax.ShapeDtypeStruct((ranks, tokens), jnp.float32),
        ),
        in_specs=[whole, whole, HBM],
        out_specs=(HBM, whole, whole),
        scratch_shapes=[
            pltpu.VMEM((tokens, width), jnp.bfloat16),
            pltpu.VMEM((ranks * cap, width), jnp.bfloat16),
            pltpu.SemaphoreType.DMA,
            pltpu.SemaphoreType.DMA((n_context,)),
        ],
        compiler_params=pltpu.CompilerParams(vmem_limit_bytes=VMEM),
        name="head",
    )(routes.T, route_weight.T, grad_out)


def times_transposed(rows, blocks):
    count, units, depth = blocks.shape
    total = None
    for i in range(count):
        part = lax.dot_general(
            rows[:, i * depth : (i + 1) * depth],
            blocks[i],
            (((1,), (1,)), ((), ())),
            preferred_element_type=jnp.float32,
        )
        total = part if total is None else total + part
    return total


def own_kernel(received_hbm, weight_hbm, out_ref, rows, weight, sems):
    loads = [
        pltpu.make_async_copy(received_hbm.at[:, pl.ds(0, rows.shape[1])], rows, sems.at[0]),
        pltpu.make_async_copy(weight_hbm, weight, sems.at[1]),
    ]
    for load in loads:
        load.start()
    for load in loads:
        load.wait()
    out_ref[...] = times_transposed(rows, weight)


def own_part(received, weight):
    count, units, depth = weight.shape
    slots = received.shape[0]
    return pl.pallas_call(
        own_kernel,
        out_shape=jax.ShapeDtypeStruct((slots, units), jnp.float32),
        in_specs=[HBM, HBM],
        scratch_shapes=[
            pltpu.VMEM((slots, count * depth), jnp.bfloat16),
            pltpu.VMEM((count, units, depth), jnp.bfloat16),
            pltpu.SemaphoreType.DMA((2,)),
        ],
        cost_estimate=pl.CostEstimate(flops=2 * 10**10, bytes_accessed=4 * 2**20, transcendentals=0),
        compiler_params=pltpu.CompilerParams(vmem_limit_bytes=VMEM),
        name="own_part",
    )(received, weight)


def project_kernel(cap, received_hbm, weight_hbm, hidden_hbm, part_hbm, slot_weight_ref, back_ref, crossing_ref, rows, weight, hidden, part, sems):
    n_context = weight_hbm.shape[0]
    slots, units = hidden.shape
    ranks = slots // cap
    c = lax.axis_index("context")
    width = rows.shape[2]
    loads = []
    for j in range(1, n_context):
        pair = (
            pltpu.make_async_copy(received_hbm.at[:, pl.ds(j * width, width)], rows.at[j - 1], sems.at[0, j - 1]),
            pltpu.make_async_copy(weight_hbm.at[lax.rem(c + j, n_context)], weight.at[j - 1], sems.at[1, j - 1]),
        )
        for load in pair:
            load.start()
        loads.append(pair)
    late = (
        pltpu.make_async_copy(hidden_hbm, hidden, sems.at[0, n_context - 1]),
        pltpu.make_async_copy(part_hbm, part, sems.at[1, n_context - 1]),
    )
    for load in late:
        load.start()
    total = None
    for j, pair in enumerate(loads):
        for load in pair:
            load.wait()
        product = times_transposed(rows.at[j], weight.at[j])
        total = product if total is None else total + product
    for load in late:
        load.wait()
    total = total + part[...]
    back_ref[...] = total
    grads = hidden[...].astype(jnp.float32) * total
    crossing_ref[:, :cap] = jnp.sum(grads.reshape(ranks, cap, units), axis=2)
    crossing_ref[:, cap:] = slot_weight_ref[...]


def project(received, weight, hidden, part, slot_weight):
    n_context, n_dp, units, depth = weight.shape
    slots = received.shape[0]
    ranks, cap = slot_weight.shape

    def kernel(*refs):
        project_kernel(cap, *refs)

    whole = pl.BlockSpec(memory_space=pltpu.VMEM)
    return pl.pallas_call(
        kernel,
        out_shape=(
            jax.ShapeDtypeStruct((slots, units), jnp.float32),
            jax.ShapeDtypeStruct((ranks, 2 * cap), jnp.float32),
        ),
        in_specs=[HBM, HBM, HBM, HBM, whole],
        scratch_shapes=[
            pltpu.VMEM((n_context - 1, slots, n_dp * depth), jnp.bfloat16),
            pltpu.VMEM((n_context - 1, n_dp, units, depth), jnp.bfloat16),
            pltpu.VMEM((slots, units), jnp.bfloat16),
            pltpu.VMEM((slots, units), jnp.float32),
            pltpu.SemaphoreType.DMA((2, n_context)),
        ],
        compiler_params=pltpu.CompilerParams(vmem_limit_bytes=VMEM),
        name="project",
    )(received, weight, hidden, part, slot_weight)


def finish_kernel(routes_ref, slot_ref, crossing_ref, gate_ref, up_ref, grad_gate_ref, grad_up_ref, out_ref):
    ranks = crossing_ref.shape[0]
    cap = crossing_ref.shape[1] // 2
    slots = ranks * cap
    topk, tokens = routes_ref.shape
    slot = slot_ref[...]
    grads = jnp.zeros((ranks, tokens), jnp.float32)
    for j in range(cap):
        grads = grads + jnp.where(slot == float(j), crossing_ref[:, j : j + 1], 0.0)
    served = served_experts(ranks, tokens)
    for k in range(topk):
        hit = routes_ref[k : k + 1, :] == served
        out_ref[k : k + 1, :] = jnp.sum(jnp.where(hit, grads, 0.0), axis=0, keepdims=True)
    row = lax.broadcasted_iota(jnp.int32, (slots, ranks), 0)
    owner = row // cap == lax.broadcasted_iota(jnp.int32, (slots, ranks), 1)
    spread = jnp.dot(
        jnp.where(owner, 1.0, 0.0).astype(jnp.bfloat16),
        crossing_ref[:, cap:].astype(jnp.bfloat16),
        preferred_element_type=jnp.float32,
    )
    mine = lax.broadcasted_iota(jnp.int32, (slots, cap), 0) % cap == lax.broadcasted_iota(
        jnp.int32, (slots, cap), 1
    )
    weight = jnp.sum(jnp.where(mine, spread, 0.0), axis=1, keepdims=True)
    grad_gate_ref[...] = (weight * gate_ref[...]).astype(jnp.bfloat16)
    grad_up_ref[...] = (weight * up_ref[...]).astype(jnp.bfloat16)


def finish(routes, slot, crossing, gate, up):
    out = jax.ShapeDtypeStruct(gate.shape, jnp.bfloat16)
    return pl.pallas_call(
        finish_kernel,
        out_shape=(out, out, jax.ShapeDtypeStruct((routes.shape[1], routes.shape[0]), jnp.float32)),
        compiler_params=pltpu.CompilerParams(vmem_limit_bytes=24 * 2**20),
        name="finish",
    )(routes.T, slot, crossing, gate, up)


def body(grad_out, routes, route_weight, saved_gate, saved_up, down_weight):
    ranks = lax.axis_size("expert")
    n_dp, n_context = lax.axis_size("dp"), lax.axis_size("context")
    cap, units = saved_gate.shape[4:]
    slots = ranks * cap
    width = grad_out.shape[1]

    over_dp = lax.all_gather(down_weight[0], "dp", axis=0, tiled=False)
    weight = lax.all_gather(over_dp, "context", axis=0, tiled=False)

    sent, slot_weight, slot = head(routes, route_weight, grad_out, ranks, cap, n_dp, n_context)
    received = lax.all_to_all(
        sent.reshape(ranks, cap, width), "expert", split_axis=0, concat_axis=0, tiled=True
    ).reshape(slots, width)

    gate = saved_gate.reshape(slots, units).astype(jnp.float32)
    up = saved_up.reshape(slots, units).astype(jnp.float32)
    sigma = jax.nn.sigmoid(gate)
    hidden = lax.optimization_barrier((gate * sigma * up).astype(jnp.bfloat16))
    part = own_part(received, over_dp)
    back, crossing = project(received, weight, hidden, part, slot_weight)
    crossing = lax.all_to_all(crossing, "expert", split_axis=0, concat_axis=0, tiled=True)
    by_gate = back * up * sigma * (1.0 + gate * (1.0 - sigma))
    by_up = back * gate * sigma
    grad_gate, grad_up, grad_weight = finish(routes, slot, crossing, by_gate, by_up)
    return grad_gate.reshape(saved_gate.shape), grad_up.reshape(saved_up.shape), grad_weight.T


def solution(mesh):
    tokens = P(("dp", "expert", "context"), None)
    saved = P("dp", "expert", "context", None, None, None)
    return jax.shard_map(
        body,
        mesh=mesh,
        in_specs=(tokens, tokens, tokens, saved, saved, P("expert", None, ("dp", "context"))),
        out_specs=(saved, saved, tokens),
        check_vma=False,
    )
```

```python
import jax
import jax.numpy as jnp
from jax import lax
from jax.experimental import pallas as pl
from jax.experimental.pallas import tpu as pltpu
from jax.sharding import PartitionSpec as P

EXPERTS = 128
VMEM = 60 * 2**20
HBM = pl.BlockSpec(memory_space=pltpu.HBM)


def served_experts(ranks, tokens):
    return lax.broadcasted_iota(jnp.int32, (ranks, tokens), 0) * (EXPERTS // ranks)


def head_kernel(ranks, cap, n_dp, n_context, routes_ref, weight_ref, grad_hbm, sent_hbm, slot_weight_ref, slot_ref, grad, sent, grad_sem, sent_sem):
    topk, tokens = routes_ref.shape
    slots = ranks * cap
    load = pltpu.make_async_copy(grad_hbm, grad, grad_sem)
    load.start()
    served = served_experts(ranks, tokens)
    hits = jnp.zeros((ranks, tokens), jnp.float32)
    picked = jnp.zeros((ranks, tokens), jnp.float32)
    for k in range(topk):
        hit = routes_ref[k : k + 1, :] == served
        hits = hits + jnp.where(hit, 1.0, 0.0)
        picked = picked + jnp.where(hit, weight_ref[k : k + 1, :].astype(jnp.float32), 0.0)
    earlier = lax.broadcasted_iota(jnp.int32, (tokens, tokens), 0) < lax.broadcasted_iota(
        jnp.int32, (tokens, tokens), 1
    )
    earlier = jnp.where(earlier, 1.0, 0.0).astype(jnp.bfloat16)
    before = jnp.dot(hits.astype(jnp.bfloat16), earlier, preferred_element_type=jnp.float32)
    slot = jnp.where(hits > 0.0, before, -1.0)
    slot_ref[...] = slot
    wide = jnp.broadcast_to(slot[:, None, :], (ranks, cap, tokens))
    place = lax.broadcasted_iota(jnp.int32, (ranks, cap, tokens), 1).astype(jnp.float32)
    choose = jnp.where(wide == place, 1.0, 0.0).reshape(slots, tokens).astype(jnp.bfloat16)
    load.wait()
    a = lax.axis_index("dp")
    c = lax.axis_index("context")
    cols = grad.shape[1] // (n_dp * n_context)
    group = n_dp * cols
    stores = []
    for j in range(n_context):
        for i in range(n_dp):
            block = lax.rem(a + i, n_dp) * n_context + lax.rem(c + j, n_context)
            part = grad[:, pl.ds(pl.multiple_of(block * cols, cols), cols)]
            at = j * group + i * cols
            out = jnp.dot(choose, part, preferred_element_type=jnp.float32)
            sent[:, at : at + cols] = out.astype(jnp.bfloat16)
        where = pl.ds(j * group, group)
        store = pltpu.make_async_copy(sent.at[:, where], sent_hbm.at[:, where], sent_sem.at[j])
        store.start()
        stores.append(store)
    lane = lax.broadcasted_iota(jnp.int32, (ranks, cap), 1).astype(jnp.float32)
    found = jnp.zeros((ranks, cap), jnp.float32)
    for j in range(cap):
        one = jnp.sum(jnp.where(slot == float(j), picked, 0.0), axis=1, keepdims=True)
        found = jnp.where(lane == float(j), one, found)
    slot_weight_ref[...] = found
    for store in stores:
        store.wait()


def head(routes, route_weight, grad_out, ranks, cap, n_dp, n_context):
    tokens, width = grad_out.shape

    def kernel(*refs):
        head_kernel(ranks, cap, n_dp, n_context, *refs)

    whole = pl.BlockSpec(memory_space=pltpu.VMEM)
    return pl.pallas_call(
        kernel,
        out_shape=(
            jax.ShapeDtypeStruct((ranks * cap, width), jnp.bfloat16),
            jax.ShapeDtypeStruct((ranks, cap), jnp.float32),
            jax.ShapeDtypeStruct((ranks, tokens), jnp.float32),
        ),
        in_specs=[whole, whole, HBM],
        out_specs=(HBM, whole, whole),
        scratch_shapes=[
            pltpu.VMEM((tokens, width), jnp.bfloat16),
            pltpu.VMEM((ranks * cap, width), jnp.bfloat16),
            pltpu.SemaphoreType.DMA,
            pltpu.SemaphoreType.DMA((n_context,)),
        ],
        compiler_params=pltpu.CompilerParams(vmem_limit_bytes=VMEM),
        name="head",
    )(routes.T, route_weight.T, grad_out)


def arrived(groups):
    def kernel(first, *refs):
        *_, out_ref, sem = refs
        copy = pltpu.make_async_copy(first.at[0, pl.ds(0, 16), pl.ds(0, 128)], out_ref, sem)
        copy.start()
        copy.wait()

    return pl.pallas_call(
        kernel,
        out_shape=jax.ShapeDtypeStruct((16, 128), groups[0].dtype),
        in_specs=[HBM] * len(groups),
        scratch_shapes=[pltpu.SemaphoreType.DMA],
        cost_estimate=pl.CostEstimate(flops=int(65e9), bytes_accessed=4096, transcendentals=0),
        compiler_params=pltpu.CompilerParams(vmem_limit_bytes=VMEM),
        name="arrived",
    )(*groups)


def project_kernel(cap, received_hbm, *refs):
    *groups, hidden_hbm, slot_weight_ref, _, back_ref, crossing_ref, rows, weight, hidden, sems = refs
    slots, units = hidden.shape
    width = rows.shape[2]
    loads = []
    for j, group in enumerate(groups):
        depth = group.shape[2]
        part = [pltpu.make_async_copy(received_hbm.at[:, pl.ds(j * width, width)], rows.at[j], sems.at[j, 0])]
        for i in range(group.shape[0]):
            side = weight.at[j, :, pl.ds(i * depth, depth)]
            part.append(pltpu.make_async_copy(group.at[i], side, sems.at[j, 1 + i]))
        for load in part:
            load.start()
        loads.append(part)
    late = pltpu.make_async_copy(hidden_hbm, hidden, sems.at[len(groups), 0])
    late.start()
    back = None
    for j, part in enumerate(loads):
        for load in part:
            load.wait()
        product = lax.dot_general(
            rows[j], weight[j], (((1,), (1,)), ((), ())), preferred_element_type=jnp.float32
        )
        back = product if back is None else back + product
    back_ref[...] = back
    late.wait()
    grads = hidden[...].astype(jnp.float32) * back
    crossing_ref[:, :cap] = jnp.sum(grads.reshape(slots // cap, cap, units), axis=2)
    crossing_ref[:, cap:] = slot_weight_ref[...]


def project(received, groups, hidden, slot_weight, tile):
    slots, units = hidden.shape
    ranks, cap = slot_weight.shape
    count, _, depth = groups[0].shape

    def kernel(*refs):
        project_kernel(cap, *refs)

    whole = pl.BlockSpec(memory_space=pltpu.VMEM)
    return pl.pallas_call(
        kernel,
        out_shape=(
            jax.ShapeDtypeStruct((slots, units), jnp.float32),
            jax.ShapeDtypeStruct((ranks, 2 * cap), jnp.float32),
        ),
        in_specs=[HBM] * (len(groups) + 2) + [whole, whole],
        scratch_shapes=[
            pltpu.VMEM((len(groups), slots, count * depth), jnp.bfloat16),
            pltpu.VMEM((len(groups), units, count * depth), jnp.bfloat16),
            pltpu.VMEM((slots, units), jnp.bfloat16),
            pltpu.SemaphoreType.DMA((len(groups) + 1, 1 + count)),
        ],
        compiler_params=pltpu.CompilerParams(vmem_limit_bytes=VMEM),
        name="project",
    )(received, *groups, hidden, slot_weight, tile)


def finish_kernel(routes_ref, slot_ref, crossing_ref, gate_ref, up_ref, grad_gate_ref, grad_up_ref, out_ref):
    ranks = crossing_ref.shape[0]
    cap = crossing_ref.shape[1] // 2
    slots = ranks * cap
    topk, tokens = routes_ref.shape
    slot = slot_ref[...]
    grads = jnp.zeros((ranks, tokens), jnp.float32)
    for j in range(cap):
        grads = grads + jnp.where(slot == float(j), crossing_ref[:, j : j + 1], 0.0)
    served = served_experts(ranks, tokens)
    for k in range(topk):
        hit = routes_ref[k : k + 1, :] == served
        out_ref[k : k + 1, :] = jnp.sum(jnp.where(hit, grads, 0.0), axis=0, keepdims=True)
    row = lax.broadcasted_iota(jnp.int32, (slots, ranks), 0)
    owner = row // cap == lax.broadcasted_iota(jnp.int32, (slots, ranks), 1)
    spread = jnp.dot(
        jnp.where(owner, 1.0, 0.0).astype(jnp.bfloat16),
        crossing_ref[:, cap:].astype(jnp.bfloat16),
        preferred_element_type=jnp.float32,
    )
    mine = lax.broadcasted_iota(jnp.int32, (slots, cap), 0) % cap == lax.broadcasted_iota(
        jnp.int32, (slots, cap), 1
    )
    weight = jnp.sum(jnp.where(mine, spread, 0.0), axis=1, keepdims=True)
    grad_gate_ref[...] = (weight * gate_ref[...]).astype(jnp.bfloat16)
    grad_up_ref[...] = (weight * up_ref[...]).astype(jnp.bfloat16)


def finish(routes, slot, crossing, gate, up):
    out = jax.ShapeDtypeStruct(gate.shape, jnp.bfloat16)
    return pl.pallas_call(
        finish_kernel,
        out_shape=(out, out, jax.ShapeDtypeStruct((routes.shape[1], routes.shape[0]), jnp.float32)),
        compiler_params=pltpu.CompilerParams(vmem_limit_bytes=24 * 2**20),
        name="finish",
    )(routes.T, slot, crossing, gate, up)


def fetch(block, axis, distance):
    size = lax.axis_size(axis)
    return lax.ppermute(block, axis, [((i + distance) % size, i) for i in range(size)])


def exchange(rows, ranks):
    blocks = rows.reshape(ranks, -1, rows.shape[1])
    return lax.all_to_all(blocks, "expert", split_axis=0, concat_axis=0, tiled=True).reshape(rows.shape)


def body(grad_out, routes, route_weight, saved_gate, saved_up, down_weight):
    ranks = lax.axis_size("expert")
    n_dp, n_context = lax.axis_size("dp"), lax.axis_size("context")
    cap, units = saved_gate.shape[4:]
    slots = ranks * cap

    own = down_weight[0]
    over_dp = jnp.stack([own] + [fetch(own, "dp", n) for n in range(1, n_dp)])
    sent, slot_weight, slot = head(routes, route_weight, grad_out, ranks, cap, n_dp, n_context)
    received = exchange(sent, ranks)
    others = [fetch(over_dp, "context", n) for n in range(1, n_context)]
    tile = arrived(others)

    gate = saved_gate.reshape(slots, units).astype(jnp.float32)
    up = saved_up.reshape(slots, units).astype(jnp.float32)
    sigma = jax.nn.sigmoid(gate)
    hidden = lax.optimization_barrier((gate * sigma * up).astype(jnp.bfloat16))
    back, crossing = project(received, [over_dp] + others, hidden, slot_weight, tile)
    crossing = lax.all_to_all(crossing, "expert", split_axis=0, concat_axis=0, tiled=True)
    by_gate = back * up * sigma * (1.0 + gate * (1.0 - sigma))
    by_up = back * gate * sigma
    grad_gate, grad_up, grad_weight = finish(routes, slot, crossing, by_gate, by_up)
    return grad_gate.reshape(saved_gate.shape), grad_up.reshape(saved_up.shape), grad_weight.T


def solution(mesh):
    tokens = P(("dp", "expert", "context"), None)
    saved = P("dp", "expert", "context", None, None, None)
    return jax.shard_map(
        body,
        mesh=mesh,
        in_specs=(tokens, tokens, tokens, saved, saved, P("expert", None, ("dp", "context"))),
        out_specs=(saved, saved, tokens),
        check_vma=False,
    )
```

```python
import jax
import jax.numpy as jnp
from jax import lax
from jax.experimental import pallas as pl
from jax.experimental.pallas import tpu as pltpu
from jax.sharding import PartitionSpec as P

EXPERTS = 128
VMEM = 60 * 2**20
HBM = pl.BlockSpec(memory_space=pltpu.HBM)


def served_experts(ranks, tokens):
    return lax.broadcasted_iota(jnp.int32, (ranks, tokens), 0) * (EXPERTS // ranks)


def head_kernel(ranks, cap, n_dp, n_context, routes_ref, weight_ref, grad_hbm, sent_hbm, slot_weight_ref, slot_ref, grad, sent, grad_sem, sent_sem):
    topk, tokens = routes_ref.shape
    slots = ranks * cap
    load = pltpu.make_async_copy(grad_hbm, grad, grad_sem)
    load.start()
    served = served_experts(ranks, tokens)
    hits = jnp.zeros((ranks, tokens), jnp.float32)
    picked = jnp.zeros((ranks, tokens), jnp.float32)
    for k in range(topk):
        hit = routes_ref[k : k + 1, :] == served
        hits = hits + jnp.where(hit, 1.0, 0.0)
        picked = picked + jnp.where(hit, weight_ref[k : k + 1, :].astype(jnp.float32), 0.0)
    earlier = lax.broadcasted_iota(jnp.int32, (tokens, tokens), 0) < lax.broadcasted_iota(
        jnp.int32, (tokens, tokens), 1
    )
    earlier = jnp.where(earlier, 1.0, 0.0).astype(jnp.bfloat16)
    before = jnp.dot(hits.astype(jnp.bfloat16), earlier, preferred_element_type=jnp.float32)
    slot = jnp.where(hits > 0.0, before, -1.0)
    slot_ref[...] = slot
    wide = jnp.broadcast_to(slot[:, None, :], (ranks, cap, tokens))
    place = lax.broadcasted_iota(jnp.int32, (ranks, cap, tokens), 1).astype(jnp.float32)
    choose = jnp.where(wide == place, 1.0, 0.0).reshape(slots, tokens).astype(jnp.bfloat16)
    load.wait()
    a = lax.axis_index("dp")
    c = lax.axis_index("context")
    cols = grad.shape[1] // (n_dp * n_context)
    group = n_dp * cols
    stores = []
    for j in range(n_context):
        for i in range(n_dp):
            block = lax.bitwise_xor(a, i) * n_context + lax.rem(c + j, n_context)
            part = grad[:, pl.ds(pl.multiple_of(block * cols, cols), cols)]
            at = j * group + i * cols
            out = jnp.dot(choose, part, preferred_element_type=jnp.float32)
            sent[:, at : at + cols] = out.astype(jnp.bfloat16)
        where = pl.ds(j * group, group)
        store = pltpu.make_async_copy(sent.at[:, where], sent_hbm.at[:, where], sent_sem.at[j])
        store.start()
        stores.append(store)
    lane = lax.broadcasted_iota(jnp.int32, (ranks, cap), 1).astype(jnp.float32)
    found = jnp.zeros((ranks, cap), jnp.float32)
    for j in range(cap):
        one = jnp.sum(jnp.where(slot == float(j), picked, 0.0), axis=1, keepdims=True)
        found = jnp.where(lane == float(j), one, found)
    slot_weight_ref[...] = found
    for store in stores:
        store.wait()


def head(routes, route_weight, grad_out, ranks, cap, n_dp, n_context):
    tokens, width = grad_out.shape

    def kernel(*refs):
        head_kernel(ranks, cap, n_dp, n_context, *refs)

    whole = pl.BlockSpec(memory_space=pltpu.VMEM)
    return pl.pallas_call(
        kernel,
        out_shape=(
            jax.ShapeDtypeStruct((ranks * cap, width), jnp.bfloat16),
            jax.ShapeDtypeStruct((ranks, cap), jnp.float32),
            jax.ShapeDtypeStruct((ranks, tokens), jnp.float32),
        ),
        in_specs=[whole, whole, HBM],
        out_specs=(HBM, whole, whole),
        scratch_shapes=[
            pltpu.VMEM((tokens, width), jnp.bfloat16),
            pltpu.VMEM((ranks * cap, width), jnp.bfloat16),
            pltpu.SemaphoreType.DMA,
            pltpu.SemaphoreType.DMA((n_context,)),
        ],
        compiler_params=pltpu.CompilerParams(vmem_limit_bytes=VMEM),
        name="head",
    )(routes.T, route_weight.T, grad_out)


def arrived(groups):
    def kernel(first, *refs):
        *_, out_ref, sem = refs
        copy = pltpu.make_async_copy(first.at[0, pl.ds(0, 16), pl.ds(0, 128)], out_ref, sem)
        copy.start()
        copy.wait()

    return pl.pallas_call(
        kernel,
        out_shape=jax.ShapeDtypeStruct((16, 128), groups[0].dtype),
        in_specs=[HBM] * len(groups),
        scratch_shapes=[pltpu.SemaphoreType.DMA],
        cost_estimate=pl.CostEstimate(flops=int(55e9), bytes_accessed=4096, transcendentals=0),
        compiler_params=pltpu.CompilerParams(vmem_limit_bytes=VMEM),
        name="arrived",
    )(*groups)


def project_kernel(cap, counts, received_hbm, *refs):
    *blocks, hidden_hbm, slot_weight_ref, _, back_ref, crossing_ref, rows, weight, hidden, sems = refs
    slots, units = hidden.shape
    width = rows.shape[2]
    loads = []
    for j, count in enumerate(counts):
        part = [pltpu.make_async_copy(received_hbm.at[:, pl.ds(j * width, width)], rows.at[j], sems.at[j, 0])]
        group, blocks = blocks[:count], blocks[count:]
        sides = [(block, i) for block in group for i in range(block.shape[0])]
        for at, (block, i) in enumerate(sides):
            depth = block.shape[2]
            side = weight.at[j, :, pl.ds(at * depth, depth)]
            part.append(pltpu.make_async_copy(block.at[i], side, sems.at[j, 1 + at]))
        for load in part:
            load.start()
        loads.append(part)
    late = pltpu.make_async_copy(hidden_hbm, hidden, sems.at[len(counts), 0])
    late.start()
    back = None
    for j, part in enumerate(loads):
        for load in part:
            load.wait()
        product = lax.dot_general(
            rows[j], weight[j], (((1,), (1,)), ((), ())), preferred_element_type=jnp.float32
        )
        back = product if back is None else back + product
    back_ref[...] = back
    late.wait()
    grads = hidden[...].astype(jnp.float32) * back
    crossing_ref[:, :cap] = jnp.sum(grads.reshape(slots // cap, cap, units), axis=2)
    crossing_ref[:, cap:] = slot_weight_ref[...]


def project(received, groups, hidden, slot_weight, tile):
    slots, units = hidden.shape
    ranks, cap = slot_weight.shape
    count, _, depth = groups[0][0].shape
    counts = [len(group) for group in groups]
    blocks = [block for group in groups for block in group]

    def kernel(*refs):
        project_kernel(cap, counts, *refs)

    whole = pl.BlockSpec(memory_space=pltpu.VMEM)
    return pl.pallas_call(
        kernel,
        out_shape=(
            jax.ShapeDtypeStruct((slots, units), jnp.float32),
            jax.ShapeDtypeStruct((ranks, 2 * cap), jnp.float32),
        ),
        in_specs=[HBM] * (len(blocks) + 2) + [whole, whole],
        scratch_shapes=[
            pltpu.VMEM((len(groups), slots, count * depth), jnp.bfloat16),
            pltpu.VMEM((len(groups), units, count * depth), jnp.bfloat16),
            pltpu.VMEM((slots, units), jnp.bfloat16),
            pltpu.SemaphoreType.DMA((len(groups) + 1, 1 + count)),
        ],
        compiler_params=pltpu.CompilerParams(vmem_limit_bytes=VMEM),
        name="project",
    )(received, *blocks, hidden, slot_weight, tile)


def finish_kernel(routes_ref, slot_ref, crossing_ref, gate_ref, up_ref, grad_gate_ref, grad_up_ref, out_ref):
    ranks = crossing_ref.shape[0]
    cap = crossing_ref.shape[1] // 2
    slots = ranks * cap
    topk, tokens = routes_ref.shape
    slot = slot_ref[...]
    grads = jnp.zeros((ranks, tokens), jnp.float32)
    for j in range(cap):
        grads = grads + jnp.where(slot == float(j), crossing_ref[:, j : j + 1], 0.0)
    served = served_experts(ranks, tokens)
    for k in range(topk):
        hit = routes_ref[k : k + 1, :] == served
        out_ref[k : k + 1, :] = jnp.sum(jnp.where(hit, grads, 0.0), axis=0, keepdims=True)
    row = lax.broadcasted_iota(jnp.int32, (slots, ranks), 0)
    owner = row // cap == lax.broadcasted_iota(jnp.int32, (slots, ranks), 1)
    spread = jnp.dot(
        jnp.where(owner, 1.0, 0.0).astype(jnp.bfloat16),
        crossing_ref[:, cap:].astype(jnp.bfloat16),
        preferred_element_type=jnp.float32,
    )
    mine = lax.broadcasted_iota(jnp.int32, (slots, cap), 0) % cap == lax.broadcasted_iota(
        jnp.int32, (slots, cap), 1
    )
    weight = jnp.sum(jnp.where(mine, spread, 0.0), axis=1, keepdims=True)
    grad_gate_ref[...] = (weight * gate_ref[...]).astype(jnp.bfloat16)
    grad_up_ref[...] = (weight * up_ref[...]).astype(jnp.bfloat16)


def finish(routes, slot, crossing, gate, up):
    out = jax.ShapeDtypeStruct(gate.shape, jnp.bfloat16)
    return pl.pallas_call(
        finish_kernel,
        out_shape=(out, out, jax.ShapeDtypeStruct((routes.shape[1], routes.shape[0]), jnp.float32)),
        compiler_params=pltpu.CompilerParams(vmem_limit_bytes=24 * 2**20),
        name="finish",
    )(routes.T, slot, crossing, gate, up)


def fetch(block, axis, partner):
    return lax.ppermute(block, axis, [(partner(i), i) for i in range(lax.axis_size(axis))])


def gather_weight(own, slot):
    size = lax.axis_size("context")
    pair = jnp.concatenate([own, fetch(own, "dp", lambda i: i ^ 1)])
    pair, _ = lax.optimization_barrier((pair, slot))
    over_dp = jnp.concatenate([pair, fetch(pair, "dp", lambda i: i ^ 2)])
    after = fetch(over_dp, "context", lambda i: (i + 1) % size)
    before = fetch(over_dp, "context", lambda i: (i - 1) % size)
    low = fetch(after[:2], "context", lambda i: (i + 1) % size)
    high = fetch(before[2:], "context", lambda i: (i - 1) % size)
    return [over_dp, after, (low, high), before]


def exchange(rows, ranks):
    blocks = rows.reshape(ranks, -1, rows.shape[1])
    return lax.all_to_all(blocks, "expert", split_axis=0, concat_axis=0, tiled=True).reshape(rows.shape)


def body(grad_out, routes, route_weight, saved_gate, saved_up, down_weight):
    ranks = lax.axis_size("expert")
    n_dp, n_context = lax.axis_size("dp"), lax.axis_size("context")
    cap, units = saved_gate.shape[4:]
    slots = ranks * cap

    sent, slot_weight, slot = head(routes, route_weight, grad_out, ranks, cap, n_dp, n_context)
    received = exchange(sent, ranks)
    groups = gather_weight(down_weight, slot)
    groups = [group if isinstance(group, tuple) else (group,) for group in groups]
    tile = arrived([*groups[2], groups[1][0], groups[3][0]])

    gate = saved_gate.reshape(slots, units).astype(jnp.float32)
    up = saved_up.reshape(slots, units).astype(jnp.float32)
    sigma = jax.nn.sigmoid(gate)
    hidden = lax.optimization_barrier((gate * sigma * up).astype(jnp.bfloat16))
    back, crossing = project(received, groups, hidden, slot_weight, tile)
    crossing = lax.all_to_all(crossing, "expert", split_axis=0, concat_axis=0, tiled=True)
    by_gate = back * up * sigma * (1.0 + gate * (1.0 - sigma))
    by_up = back * gate * sigma
    grad_gate, grad_up, grad_weight = finish(routes, slot, crossing, by_gate, by_up)
    return grad_gate.reshape(saved_gate.shape), grad_up.reshape(saved_up.shape), grad_weight.T


def solution(mesh):
    tokens = P(("dp", "expert", "context"), None)
    saved = P("dp", "expert", "context", None, None, None)
    return jax.shard_map(
        body,
        mesh=mesh,
        in_specs=(tokens, tokens, tokens, saved, saved, P("expert", None, ("dp", "context"))),
        out_specs=(saved, saved, tokens),
        check_vma=False,
    )
```

```python
import jax
import jax.numpy as jnp
from jax import lax
from jax.experimental import pallas as pl
from jax.experimental.pallas import tpu as pltpu
from jax.sharding import PartitionSpec as P

EXPERTS = 128
VMEM = 60 * 2**20
HBM = pl.BlockSpec(memory_space=pltpu.HBM)


def served_experts(ranks, tokens):
    return lax.broadcasted_iota(jnp.int32, (ranks, tokens), 0) * (EXPERTS // ranks)


def head_kernel(ranks, cap, n_dp, n_context, routes_ref, weight_ref, grad_hbm, sent_hbm, slot_weight_ref, slot_ref, grad, sent, grad_sem, sent_sem):
    topk, tokens = routes_ref.shape
    slots = ranks * cap
    load = pltpu.make_async_copy(grad_hbm, grad, grad_sem)
    load.start()
    served = served_experts(ranks, tokens)
    hits = jnp.zeros((ranks, tokens), jnp.float32)
    picked = jnp.zeros((ranks, tokens), jnp.float32)
    for k in range(topk):
        hit = routes_ref[k : k + 1, :] == served
        hits = hits + jnp.where(hit, 1.0, 0.0)
        picked = picked + jnp.where(hit, weight_ref[k : k + 1, :].astype(jnp.float32), 0.0)
    earlier = lax.broadcasted_iota(jnp.int32, (tokens, tokens), 0) < lax.broadcasted_iota(
        jnp.int32, (tokens, tokens), 1
    )
    earlier = jnp.where(earlier, 1.0, 0.0).astype(jnp.bfloat16)
    before = jnp.dot(hits.astype(jnp.bfloat16), earlier, preferred_element_type=jnp.float32)
    slot = jnp.where(hits > 0.0, before, -1.0)
    slot_ref[...] = slot
    wide = jnp.broadcast_to(slot[:, None, :], (ranks, cap, tokens))
    place = lax.broadcasted_iota(jnp.int32, (ranks, cap, tokens), 1).astype(jnp.float32)
    choose = jnp.where(wide == place, 1.0, 0.0).reshape(slots, tokens).astype(jnp.bfloat16)
    load.wait()
    a = lax.axis_index("dp")
    c = lax.axis_index("context")
    cols = grad.shape[1] // (n_dp * n_context)
    group = n_dp * cols
    stores = []
    for j in range(n_context):
        for i in range(n_dp):
            block = lax.rem(a + i, n_dp) * n_context + lax.rem(c + j, n_context)
            part = grad[:, pl.ds(pl.multiple_of(block * cols, cols), cols)]
            at = j * group + i * cols
            out = jnp.dot(choose, part, preferred_element_type=jnp.float32)
            sent[:, at : at + cols] = out.astype(jnp.bfloat16)
        where = pl.ds(j * group, group)
        store = pltpu.make_async_copy(sent.at[:, where], sent_hbm.at[:, where], sent_sem.at[j])
        store.start()
        stores.append(store)
    lane = lax.broadcasted_iota(jnp.int32, (ranks, cap), 1).astype(jnp.float32)
    found = jnp.zeros((ranks, cap), jnp.float32)
    for j in range(cap):
        one = jnp.sum(jnp.where(slot == float(j), picked, 0.0), axis=1, keepdims=True)
        found = jnp.where(lane == float(j), one, found)
    slot_weight_ref[...] = found
    for store in stores:
        store.wait()


def head(routes, route_weight, grad_out, ranks, cap, n_dp, n_context):
    tokens, width = grad_out.shape

    def kernel(*refs):
        head_kernel(ranks, cap, n_dp, n_context, *refs)

    whole = pl.BlockSpec(memory_space=pltpu.VMEM)
    return pl.pallas_call(
        kernel,
        out_shape=(
            jax.ShapeDtypeStruct((ranks * cap, width), jnp.bfloat16),
            jax.ShapeDtypeStruct((ranks, cap), jnp.float32),
            jax.ShapeDtypeStruct((ranks, tokens), jnp.float32),
        ),
        in_specs=[whole, whole, HBM],
        out_specs=(HBM, whole, whole),
        scratch_shapes=[
            pltpu.VMEM((tokens, width), jnp.bfloat16),
            pltpu.VMEM((ranks * cap, width), jnp.bfloat16),
            pltpu.SemaphoreType.DMA,
            pltpu.SemaphoreType.DMA((n_context,)),
        ],
        compiler_params=pltpu.CompilerParams(vmem_limit_bytes=VMEM),
        name="head",
    )(routes.T, route_weight.T, grad_out)


def arrived(groups):
    def kernel(first, *refs):
        *_, out_ref, sem = refs
        copy = pltpu.make_async_copy(first.at[0, pl.ds(0, 16), pl.ds(0, 128)], out_ref, sem)
        copy.start()
        copy.wait()

    return pl.pallas_call(
        kernel,
        out_shape=jax.ShapeDtypeStruct((16, 128), groups[0].dtype),
        in_specs=[HBM] * len(groups),
        scratch_shapes=[pltpu.SemaphoreType.DMA],
        cost_estimate=pl.CostEstimate(flops=int(5e10), bytes_accessed=4096, transcendentals=0),
        compiler_params=pltpu.CompilerParams(vmem_limit_bytes=VMEM),
        name="arrived",
    )(*groups)


def project_kernel(cap, counts, received_hbm, *refs):
    *blocks, hidden_hbm, slot_weight_ref, _, back_hbm, crossing_ref, rows, weight, hidden, back, sems = refs
    first = blocks[0]
    depth = first.shape[2]
    slots, units = hidden.shape
    width = rows.shape[2]
    way = turn(lax.axis_index("expert"))
    for j, count in enumerate(counts):
        part = [pltpu.make_async_copy(received_hbm.at[:, pl.ds(j * width, width)], rows.at[j], sems.at[j, 0])]
        group, blocks = blocks[:count], blocks[count:]
        sides = [(block, i) for block in group for i in range(block.shape[0])]
        for at, (block, i) in enumerate(sides):
            place = lax.rem(len(sides) + at * way, len(sides)) * depth
            side = weight.at[j, :, pl.ds(pl.multiple_of(place, depth), depth)]
            part.append(pltpu.make_async_copy(block.at[i], side, sems.at[j, 1 + at]))
        for load in part:
            load.start()
    late = pltpu.make_async_copy(hidden_hbm, hidden, sems.at[len(counts), 0])
    late.start()
    back[...] = jnp.zeros_like(back)

    def add(j, _):
        pltpu.make_async_copy(received_hbm.at[:, pl.ds(0, width)], rows.at[j], sems.at[j, 0]).wait()
        for at in range(width // depth):
            side = weight.at[j, :, pl.ds(at * depth, depth)]
            pltpu.make_async_copy(first.at[0], side, sems.at[j, 1 + at]).wait()
        back[...] += lax.dot_general(
            rows[j], weight[j], (((1,), (1,)), ((), ())), preferred_element_type=jnp.float32
        )
        return 0

    lax.fori_loop(0, len(counts), add, 0)
    store = pltpu.make_async_copy(back, back_hbm, sems.at[len(counts), 1])
    store.start()
    late.wait()
    tall = 128

    def reduce(t, _):
        some = pl.ds(pl.multiple_of(t * tall, tall), tall)
        grads = hidden[some, :].astype(jnp.float32) * back[some, :]
        few = pl.ds(pl.multiple_of(t * (tall // cap), tall // cap), tall // cap)
        crossing_ref[few, :cap] = jnp.sum(grads.reshape(tall // cap, cap, units), axis=2)
        return 0

    lax.fori_loop(0, slots // tall, reduce, 0)
    crossing_ref[:, cap:] = slot_weight_ref[...]
    store.wait()


def project(received, groups, hidden, slot_weight, tile):
    slots, units = hidden.shape
    ranks, cap = slot_weight.shape
    count, _, depth = groups[0][0].shape
    counts = [len(group) for group in groups]
    blocks = [block for group in groups for block in group]

    def kernel(*refs):
        project_kernel(cap, counts, *refs)

    whole = pl.BlockSpec(memory_space=pltpu.VMEM)
    return pl.pallas_call(
        kernel,
        out_shape=(
            jax.ShapeDtypeStruct((slots, units), jnp.float32),
            jax.ShapeDtypeStruct((ranks, 2 * cap), jnp.float32),
        ),
        in_specs=[HBM] * (len(blocks) + 2) + [whole, whole],
        out_specs=(HBM, whole),
        scratch_shapes=[
            pltpu.VMEM((len(groups), slots, count * depth), jnp.bfloat16),
            pltpu.VMEM((len(groups), units, count * depth), jnp.bfloat16),
            pltpu.VMEM((slots, units), jnp.bfloat16),
            pltpu.VMEM((slots, units), jnp.float32),
            pltpu.SemaphoreType.DMA((len(groups) + 1, 1 + count)),
        ],
        compiler_params=pltpu.CompilerParams(vmem_limit_bytes=VMEM),
        name="project",
    )(received, *blocks, hidden, slot_weight, tile)


def finish_kernel(routes_ref, slot_ref, crossing_ref, gate_ref, up_ref, grad_gate_ref, grad_up_ref, out_ref):
    ranks = crossing_ref.shape[0]
    cap = crossing_ref.shape[1] // 2
    slots = ranks * cap
    topk, tokens = routes_ref.shape
    slot = slot_ref[...]
    grads = jnp.zeros((ranks, tokens), jnp.float32)
    for j in range(cap):
        grads = grads + jnp.where(slot == float(j), crossing_ref[:, j : j + 1], 0.0)
    served = served_experts(ranks, tokens)
    for k in range(topk):
        hit = routes_ref[k : k + 1, :] == served
        out_ref[k : k + 1, :] = jnp.sum(jnp.where(hit, grads, 0.0), axis=0, keepdims=True)
    row = lax.broadcasted_iota(jnp.int32, (slots, ranks), 0)
    owner = row // cap == lax.broadcasted_iota(jnp.int32, (slots, ranks), 1)
    spread = jnp.dot(
        jnp.where(owner, 1.0, 0.0).astype(jnp.bfloat16),
        crossing_ref[:, cap:].astype(jnp.bfloat16),
        preferred_element_type=jnp.float32,
    )
    mine = lax.broadcasted_iota(jnp.int32, (slots, cap), 0) % cap == lax.broadcasted_iota(
        jnp.int32, (slots, cap), 1
    )
    weight = jnp.sum(jnp.where(mine, spread, 0.0), axis=1, keepdims=True)
    grad_gate_ref[...] = (weight * gate_ref[...]).astype(jnp.bfloat16)
    grad_up_ref[...] = (weight * up_ref[...]).astype(jnp.bfloat16)


def finish(routes, slot, crossing, gate, up):
    out = jax.ShapeDtypeStruct(gate.shape, jnp.bfloat16)
    return pl.pallas_call(
        finish_kernel,
        out_shape=(out, out, jax.ShapeDtypeStruct((routes.shape[1], routes.shape[0]), jnp.float32)),
        compiler_params=pltpu.CompilerParams(vmem_limit_bytes=24 * 2**20),
        name="finish",
    )(routes.T, slot, crossing, gate, up)


def fetch(block, axis, partner):
    return lax.ppermute(block, axis, [(partner(i), i) for i in range(lax.axis_size(axis))])


def turn(expert):
    return 1 - 2 * ((expert // 2) % 2)


def fetch_next(block):
    n_dp, ranks = lax.axis_size("dp"), lax.axis_size("expert")
    pairs = [((a + turn(b)) % n_dp * ranks + b, a * ranks + b) for a in range(n_dp) for b in range(ranks)]
    return lax.ppermute(block, ("dp", "expert"), pairs)


def gather_weight(own):
    size = lax.axis_size("context")
    blocks = [own]
    for _ in range(lax.axis_size("dp") - 1):
        blocks.append(fetch_next(blocks[-1]))
    over_dp = jnp.concatenate(blocks)
    after = fetch(over_dp, "context", lambda i: (i + 1) % size)
    before = fetch(over_dp, "context", lambda i: (i - 1) % size)
    low = fetch(after[:2], "context", lambda i: (i + 1) % size)
    high = fetch(before[2:], "context", lambda i: (i - 1) % size)
    return [over_dp, after, (low, high), before]


def exchange(rows, ranks):
    blocks = rows.reshape(ranks, -1, rows.shape[1])
    return lax.all_to_all(blocks, "expert", split_axis=0, concat_axis=0, tiled=True).reshape(rows.shape)


def body(grad_out, routes, route_weight, saved_gate, saved_up, down_weight):
    ranks = lax.axis_size("expert")
    n_dp, n_context = lax.axis_size("dp"), lax.axis_size("context")
    cap, units = saved_gate.shape[4:]
    slots = ranks * cap

    sent, slot_weight, slot = head(routes, route_weight, grad_out, ranks, cap, n_dp, n_context)
    received = exchange(sent, ranks)
    groups = gather_weight(down_weight)
    groups = [group if isinstance(group, tuple) else (group,) for group in groups]
    tile = arrived([*groups[2], groups[1][0], groups[3][0]])

    gate = saved_gate.reshape(slots, units).astype(jnp.float32)
    up = saved_up.reshape(slots, units).astype(jnp.float32)
    sigma = jax.nn.sigmoid(gate)
    hidden = lax.optimization_barrier((gate * sigma * up).astype(jnp.bfloat16))
    back, crossing = project(received, groups, hidden, slot_weight, tile)
    crossing = lax.all_to_all(crossing, "expert", split_axis=0, concat_axis=0, tiled=True)
    by_gate = back * up * sigma * (1.0 + gate * (1.0 - sigma))
    by_up = back * gate * sigma
    grad_gate, grad_up, grad_weight = finish(routes, slot, crossing, by_gate, by_up)
    return grad_gate.reshape(saved_gate.shape), grad_up.reshape(saved_up.shape), grad_weight.T


def solution(mesh):
    tokens = P(("dp", "expert", "context"), None)
    saved = P("dp", "expert", "context", None, None, None)
    return jax.shard_map(
        body,
        mesh=mesh,
        in_specs=(tokens, tokens, tokens, saved, saved, P("expert", None, ("dp", "context"))),
        out_specs=(saved, saved, tokens),
        check_vma=False,
    )
```

```python
import jax
import jax.numpy as jnp
from jax import lax
from jax.experimental import pallas as pl
from jax.experimental.pallas import tpu as pltpu
from jax.sharding import PartitionSpec as P

EXPERTS = 128
VMEM = 60 * 2**20
HBM = pl.BlockSpec(memory_space=pltpu.HBM)


def served_experts(ranks, tokens):
    return lax.broadcasted_iota(jnp.int32, (ranks, tokens), 0) * (EXPERTS // ranks)


def head_kernel(ranks, cap, n_dp, n_context, routes_ref, weight_ref, grad_hbm, sent_hbm, slot_weight_ref, slot_ref, grad, sent, grad_sem, sent_sem):
    topk, tokens = routes_ref.shape
    slots = ranks * cap
    load = pltpu.make_async_copy(grad_hbm, grad, grad_sem)
    load.start()
    served = served_experts(ranks, tokens)
    hits = jnp.zeros((ranks, tokens), jnp.float32)
    picked = jnp.zeros((ranks, tokens), jnp.float32)
    for k in range(topk):
        hit = routes_ref[k : k + 1, :] == served
        hits = hits + jnp.where(hit, 1.0, 0.0)
        picked = picked + jnp.where(hit, weight_ref[k : k + 1, :].astype(jnp.float32), 0.0)
    earlier = lax.broadcasted_iota(jnp.int32, (tokens, tokens), 0) < lax.broadcasted_iota(
        jnp.int32, (tokens, tokens), 1
    )
    earlier = jnp.where(earlier, 1.0, 0.0).astype(jnp.bfloat16)
    before = jnp.dot(hits.astype(jnp.bfloat16), earlier, preferred_element_type=jnp.float32)
    slot = jnp.where(hits > 0.0, before, -1.0)
    slot_ref[...] = slot
    wide = jnp.broadcast_to(slot[:, None, :], (ranks, cap, tokens))
    place = lax.broadcasted_iota(jnp.int32, (ranks, cap, tokens), 1).astype(jnp.float32)
    choose = jnp.where(wide == place, 1.0, 0.0).reshape(slots, tokens).astype(jnp.bfloat16)
    load.wait()
    a = lax.axis_index("dp")
    c = lax.axis_index("context")
    cols = grad.shape[1] // (n_dp * n_context)
    group = n_dp * cols
    stores = []
    for j in range(n_context):
        for i in range(n_dp):
            block = lax.rem(a + i, n_dp) * n_context + lax.rem(c + j, n_context)
            part = grad[:, pl.ds(pl.multiple_of(block * cols, cols), cols)]
            at = j * group + i * cols
            out = jnp.dot(choose, part, preferred_element_type=jnp.float32)
            sent[:, at : at + cols] = out.astype(jnp.bfloat16)
        where = pl.ds(j * group, group)
        store = pltpu.make_async_copy(sent.at[:, where], sent_hbm.at[:, where], sent_sem.at[j])
        store.start()
        stores.append(store)
    lane = lax.broadcasted_iota(jnp.int32, (ranks, cap), 1).astype(jnp.float32)
    found = jnp.zeros((ranks, cap), jnp.float32)
    for j in range(cap):
        one = jnp.sum(jnp.where(slot == float(j), picked, 0.0), axis=1, keepdims=True)
        found = jnp.where(lane == float(j), one, found)
    slot_weight_ref[...] = found
    for store in stores:
        store.wait()


def head(routes, route_weight, grad_out, ranks, cap, n_dp, n_context):
    tokens, width = grad_out.shape

    def kernel(*refs):
        head_kernel(ranks, cap, n_dp, n_context, *refs)

    whole = pl.BlockSpec(memory_space=pltpu.VMEM)
    return pl.pallas_call(
        kernel,
        out_shape=(
            jax.ShapeDtypeStruct((ranks * cap, width), jnp.bfloat16),
            jax.ShapeDtypeStruct((ranks, cap), jnp.float32),
            jax.ShapeDtypeStruct((ranks, tokens), jnp.float32),
        ),
        in_specs=[whole, whole, HBM],
        out_specs=(HBM, whole, whole),
        scratch_shapes=[
            pltpu.VMEM((tokens, width), jnp.bfloat16),
            pltpu.VMEM((ranks * cap, width), jnp.bfloat16),
            pltpu.SemaphoreType.DMA,
            pltpu.SemaphoreType.DMA((n_context,)),
        ],
        compiler_params=pltpu.CompilerParams(vmem_limit_bytes=VMEM),
        name="head",
    )(routes.T, route_weight.T, grad_out)


def project_kernel(cap, counts, received_hbm, *refs):
    *blocks, hidden_hbm, slot_weight_ref, back_hbm, crossing_ref, rows, weight, hidden, back, sems = refs
    first = blocks[0]
    depth = first.shape[2]
    slots, units = hidden.shape
    width = rows.shape[2]
    way = turn(lax.axis_index("expert"))
    for j, count in enumerate(counts):
        part = [pltpu.make_async_copy(received_hbm.at[:, pl.ds(j * width, width)], rows.at[j], sems.at[j, 0])]
        group, blocks = blocks[:count], blocks[count:]
        sides = [(block, i) for block in group for i in range(block.shape[0])]
        for at, (block, i) in enumerate(sides):
            place = lax.rem(len(sides) + at * way, len(sides)) * depth
            side = weight.at[j, :, pl.ds(pl.multiple_of(place, depth), depth)]
            part.append(pltpu.make_async_copy(block.at[i], side, sems.at[j, 1 + at]))
        for load in part:
            load.start()
    late = pltpu.make_async_copy(hidden_hbm, hidden, sems.at[len(counts), 0])
    late.start()
    back[...] = jnp.zeros_like(back)

    def add(j, _):
        pltpu.make_async_copy(received_hbm.at[:, pl.ds(0, width)], rows.at[j], sems.at[j, 0]).wait()
        for at in range(width // depth):
            side = weight.at[j, :, pl.ds(at * depth, depth)]
            pltpu.make_async_copy(first.at[0], side, sems.at[j, 1 + at]).wait()
        back[...] += lax.dot_general(
            rows[j], weight[j], (((1,), (1,)), ((), ())), preferred_element_type=jnp.float32
        )
        return 0

    lax.fori_loop(0, len(counts), add, 0)
    store = pltpu.make_async_copy(back, back_hbm, sems.at[len(counts), 1])
    store.start()
    late.wait()
    tall = 128

    def reduce(t, _):
        some = pl.ds(pl.multiple_of(t * tall, tall), tall)
        grads = hidden[some, :].astype(jnp.float32) * back[some, :]
        few = pl.ds(pl.multiple_of(t * (tall // cap), tall // cap), tall // cap)
        crossing_ref[few, :cap] = jnp.sum(grads.reshape(tall // cap, cap, units), axis=2)
        return 0

    lax.fori_loop(0, slots // tall, reduce, 0)
    crossing_ref[:, cap:] = slot_weight_ref[...]
    store.wait()


def project(received, groups, hidden, slot_weight):
    slots, units = hidden.shape
    ranks, cap = slot_weight.shape
    depth = groups[0][0].shape[2]
    count = sum(block.shape[0] for block in groups[0])
    counts = [len(group) for group in groups]
    blocks = [block for group in groups for block in group]

    def kernel(*refs):
        project_kernel(cap, counts, *refs)

    whole = pl.BlockSpec(memory_space=pltpu.VMEM)
    return pl.pallas_call(
        kernel,
        out_shape=(
            jax.ShapeDtypeStruct((slots, units), jnp.float32),
            jax.ShapeDtypeStruct((ranks, 2 * cap), jnp.float32),
        ),
        in_specs=[HBM] * (len(blocks) + 2) + [whole],
        out_specs=(HBM, whole),
        scratch_shapes=[
            pltpu.VMEM((len(groups), slots, count * depth), jnp.bfloat16),
            pltpu.VMEM((len(groups), units, count * depth), jnp.bfloat16),
            pltpu.VMEM((slots, units), jnp.bfloat16),
            pltpu.VMEM((slots, units), jnp.float32),
            pltpu.SemaphoreType.DMA((len(groups) + 1, 1 + count)),
        ],
        compiler_params=pltpu.CompilerParams(vmem_limit_bytes=VMEM),
        name="project",
    )(received, *blocks, hidden, slot_weight)


def finish_kernel(routes_ref, slot_ref, crossing_ref, gate_ref, up_ref, grad_gate_ref, grad_up_ref, out_ref):
    ranks = crossing_ref.shape[0]
    cap = crossing_ref.shape[1] // 2
    slots = ranks * cap
    topk, tokens = routes_ref.shape
    slot = slot_ref[...]
    grads = jnp.zeros((ranks, tokens), jnp.float32)
    for j in range(cap):
        grads = grads + jnp.where(slot == float(j), crossing_ref[:, j : j + 1], 0.0)
    served = served_experts(ranks, tokens)
    for k in range(topk):
        hit = routes_ref[k : k + 1, :] == served
        out_ref[k : k + 1, :] = jnp.sum(jnp.where(hit, grads, 0.0), axis=0, keepdims=True)
    row = lax.broadcasted_iota(jnp.int32, (slots, ranks), 0)
    owner = row // cap == lax.broadcasted_iota(jnp.int32, (slots, ranks), 1)
    spread = jnp.dot(
        jnp.where(owner, 1.0, 0.0).astype(jnp.bfloat16),
        crossing_ref[:, cap:].astype(jnp.bfloat16),
        preferred_element_type=jnp.float32,
    )
    mine = lax.broadcasted_iota(jnp.int32, (slots, cap), 0) % cap == lax.broadcasted_iota(
        jnp.int32, (slots, cap), 1
    )
    weight = jnp.sum(jnp.where(mine, spread, 0.0), axis=1, keepdims=True)
    grad_gate_ref[...] = (weight * gate_ref[...]).astype(jnp.bfloat16)
    grad_up_ref[...] = (weight * up_ref[...]).astype(jnp.bfloat16)


def finish(routes, slot, crossing, gate, up):
    out = jax.ShapeDtypeStruct(gate.shape, jnp.bfloat16)
    return pl.pallas_call(
        finish_kernel,
        out_shape=(out, out, jax.ShapeDtypeStruct((routes.shape[1], routes.shape[0]), jnp.float32)),
        compiler_params=pltpu.CompilerParams(vmem_limit_bytes=24 * 2**20),
        name="finish",
    )(routes.T, slot, crossing, gate, up)


def fetch(block, axis, partner):
    return lax.ppermute(block, axis, [(partner(i), i) for i in range(lax.axis_size(axis))])


def turn(expert):
    return 1 - 2 * ((expert // 2) % 2)


def fetch_next(block):
    n_dp, ranks = lax.axis_size("dp"), lax.axis_size("expert")
    pairs = [((a + turn(b)) % n_dp * ranks + b, a * ranks + b) for a in range(n_dp) for b in range(ranks)]
    return lax.ppermute(block, ("dp", "expert"), pairs)


def gather_weight(own):
    size = lax.axis_size("context")

    def after(block):
        return fetch(block, "context", lambda i: (i + 1) % size)

    def before(block):
        return fetch(block, "context", lambda i: (i - 1) % size)

    one = fetch_next(own)
    two = fetch_next(one)
    near = jnp.concatenate([own, one])
    near_after, near_before = after(near), before(near)
    far = jnp.concatenate([two, fetch_next(two)])
    far, near_after, near_before = lax.optimization_barrier((far, near_after, near_before))
    far_after, far_before = after(far), before(far)
    return [(near, far), (near_after, far_after), (after(near_after), before(far_before)), (near_before, far_before)]


def exchange(rows, ranks):
    blocks = rows.reshape(ranks, -1, rows.shape[1])
    return lax.all_to_all(blocks, "expert", split_axis=0, concat_axis=0, tiled=True).reshape(rows.shape)


def body(grad_out, routes, route_weight, saved_gate, saved_up, down_weight):
    ranks = lax.axis_size("expert")
    n_dp, n_context = lax.axis_size("dp"), lax.axis_size("context")
    cap, units = saved_gate.shape[4:]
    slots = ranks * cap

    sent, slot_weight, slot = head(routes, route_weight, grad_out, ranks, cap, n_dp, n_context)
    received = exchange(sent, ranks)
    groups = gather_weight(down_weight)

    gate = saved_gate.reshape(slots, units).astype(jnp.float32)
    up = saved_up.reshape(slots, units).astype(jnp.float32)
    sigma = jax.nn.sigmoid(gate)
    hidden = lax.optimization_barrier((gate * sigma * up).astype(jnp.bfloat16))
    back, crossing = project(received, groups, hidden, slot_weight)
    crossing = lax.all_to_all(crossing, "expert", split_axis=0, concat_axis=0, tiled=True)
    by_gate = back * up * sigma * (1.0 + gate * (1.0 - sigma))
    by_up = back * gate * sigma
    grad_gate, grad_up, grad_weight = finish(routes, slot, crossing, by_gate, by_up)
    return grad_gate.reshape(saved_gate.shape), grad_up.reshape(saved_up.shape), grad_weight.T


def solution(mesh):
    tokens = P(("dp", "expert", "context"), None)
    saved = P("dp", "expert", "context", None, None, None)
    return jax.shard_map(
        body,
        mesh=mesh,
        in_specs=(tokens, tokens, tokens, saved, saved, P("expert", None, ("dp", "context"))),
        out_specs=(saved, saved, tokens),
        check_vma=False,
    )
```

```python
import jax
import jax.numpy as jnp
from jax import lax
from jax.experimental import pallas as pl
from jax.experimental.pallas import tpu as pltpu
from jax.sharding import PartitionSpec as P

EXPERTS = 128
VMEM = 60 * 2**20
HBM = pl.BlockSpec(memory_space=pltpu.HBM)


def served_experts(ranks, tokens):
    return lax.broadcasted_iota(jnp.int32, (ranks, tokens), 0) * (EXPERTS // ranks)


def head_kernel(ranks, cap, n_dp, n_context, routes_ref, weight_ref, grad_hbm, sent_hbm, slot_weight_ref, slot_ref, grad, sent, grad_sem, sent_sem):
    topk, tokens = routes_ref.shape
    slots = ranks * cap
    load = pltpu.make_async_copy(grad_hbm, grad, grad_sem)
    load.start()
    served = served_experts(ranks, tokens)
    hits = jnp.zeros((ranks, tokens), jnp.float32)
    picked = jnp.zeros((ranks, tokens), jnp.float32)
    for k in range(topk):
        hit = routes_ref[k : k + 1, :] == served
        hits = hits + jnp.where(hit, 1.0, 0.0)
        picked = picked + jnp.where(hit, weight_ref[k : k + 1, :].astype(jnp.float32), 0.0)
    earlier = lax.broadcasted_iota(jnp.int32, (tokens, tokens), 0) < lax.broadcasted_iota(
        jnp.int32, (tokens, tokens), 1
    )
    earlier = jnp.where(earlier, 1.0, 0.0).astype(jnp.bfloat16)
    before = jnp.dot(hits.astype(jnp.bfloat16), earlier, preferred_element_type=jnp.float32)
    slot = jnp.where(hits > 0.0, before, -1.0)
    slot_ref[...] = slot
    wide = jnp.broadcast_to(slot[:, None, :], (ranks, cap, tokens))
    place = lax.broadcasted_iota(jnp.int32, (ranks, cap, tokens), 1).astype(jnp.float32)
    choose = jnp.where(wide == place, 1.0, 0.0).reshape(slots, tokens).astype(jnp.bfloat16)
    load.wait()
    a = lax.axis_index("dp")
    c = lax.axis_index("context")
    cols = grad.shape[1] // (n_dp * n_context)
    group = n_dp * cols
    stores = []
    for j in range(n_context):
        for i in range(n_dp):
            block = lax.rem(a + i, n_dp) * n_context + lax.rem(c + j, n_context)
            part = grad[:, pl.ds(pl.multiple_of(block * cols, cols), cols)]
            at = j * group + i * cols
            out = jnp.dot(choose, part, preferred_element_type=jnp.float32)
            sent[:, at : at + cols] = out.astype(jnp.bfloat16)
            where = pl.ds(at, cols)
            store = pltpu.make_async_copy(sent.at[:, where], sent_hbm.at[:, where], sent_sem.at[j * n_dp + i])
            store.start()
            stores.append(store)
    lane = lax.broadcasted_iota(jnp.int32, (ranks, cap), 1).astype(jnp.float32)
    found = jnp.zeros((ranks, cap), jnp.float32)
    for j in range(cap):
        one = jnp.sum(jnp.where(slot == float(j), picked, 0.0), axis=1, keepdims=True)
        found = jnp.where(lane == float(j), one, found)
    slot_weight_ref[...] = found
    for store in stores:
        store.wait()


def head(routes, route_weight, grad_out, ranks, cap, n_dp, n_context):
    tokens, width = grad_out.shape

    def kernel(*refs):
        head_kernel(ranks, cap, n_dp, n_context, *refs)

    whole = pl.BlockSpec(memory_space=pltpu.VMEM)
    return pl.pallas_call(
        kernel,
        out_shape=(
            jax.ShapeDtypeStruct((ranks * cap, width), jnp.bfloat16),
            jax.ShapeDtypeStruct((ranks, cap), jnp.float32),
            jax.ShapeDtypeStruct((ranks, tokens), jnp.float32),
        ),
        in_specs=[whole, whole, HBM],
        out_specs=(HBM, whole, whole),
        scratch_shapes=[
            pltpu.VMEM((tokens, width), jnp.bfloat16),
            pltpu.VMEM((ranks * cap, width), jnp.bfloat16),
            pltpu.SemaphoreType.DMA,
            pltpu.SemaphoreType.DMA((n_context * n_dp,)),
        ],
        compiler_params=pltpu.CompilerParams(vmem_limit_bytes=VMEM),
        name="head",
    )(routes.T, route_weight.T, grad_out)


def project_kernel(cap, counts, received_hbm, *refs):
    *blocks, hidden_hbm, slot_weight_ref, back_hbm, crossing_ref, rows, weight, hidden, back, sems = refs
    first = blocks[0]
    depth = first.shape[2]
    slots, units = hidden.shape
    width = rows.shape[2]
    way = turn(lax.axis_index("expert"))
    for j, count in enumerate(counts):
        part = [pltpu.make_async_copy(received_hbm.at[:, pl.ds(j * width, width)], rows.at[j], sems.at[j, 0])]
        group, blocks = blocks[:count], blocks[count:]
        sides = [(block, i) for block in group for i in range(block.shape[0])]
        for at, (block, i) in enumerate(sides):
            place = lax.rem(len(sides) + at * way, len(sides)) * depth
            side = weight.at[j, :, pl.ds(pl.multiple_of(place, depth), depth)]
            part.append(pltpu.make_async_copy(block.at[i], side, sems.at[j, 1 + at]))
        for load in part:
            load.start()
    late = pltpu.make_async_copy(hidden_hbm, hidden, sems.at[len(counts), 0])
    late.start()
    back[...] = jnp.zeros_like(back)

    def add(j, _):
        pltpu.make_async_copy(received_hbm.at[:, pl.ds(0, width)], rows.at[j], sems.at[j, 0]).wait()
        for at in range(width // depth):
            side = weight.at[j, :, pl.ds(at * depth, depth)]
            pltpu.make_async_copy(first.at[0], side, sems.at[j, 1 + at]).wait()
        back[...] += lax.dot_general(
            rows[j], weight[j], (((1,), (1,)), ((), ())), preferred_element_type=jnp.float32
        )
        return 0

    lax.fori_loop(0, len(counts), add, 0)
    store = pltpu.make_async_copy(back, back_hbm, sems.at[len(counts), 1])
    store.start()
    late.wait()
    tall = 128

    def reduce(t, _):
        some = pl.ds(pl.multiple_of(t * tall, tall), tall)
        grads = hidden[some, :].astype(jnp.float32) * back[some, :]
        few = pl.ds(pl.multiple_of(t * (tall // cap), tall // cap), tall // cap)
        crossing_ref[few, :cap] = jnp.sum(grads.reshape(tall // cap, cap, units), axis=2)
        return 0

    lax.fori_loop(0, slots // tall, reduce, 0)
    crossing_ref[:, cap:] = slot_weight_ref[...]
    store.wait()


def project(received, groups, hidden, slot_weight):
    slots, units = hidden.shape
    ranks, cap = slot_weight.shape
    depth = groups[0][0].shape[2]
    count = sum(block.shape[0] for block in groups[0])
    counts = [len(group) for group in groups]
    blocks = [block for group in groups for block in group]

    def kernel(*refs):
        project_kernel(cap, counts, *refs)

    whole = pl.BlockSpec(memory_space=pltpu.VMEM)
    return pl.pallas_call(
        kernel,
        out_shape=(
            jax.ShapeDtypeStruct((slots, units), jnp.float32),
            jax.ShapeDtypeStruct((ranks, 2 * cap), jnp.float32),
        ),
        in_specs=[HBM] * (len(blocks) + 2) + [whole],
        out_specs=(HBM, whole),
        scratch_shapes=[
            pltpu.VMEM((len(groups), slots, count * depth), jnp.bfloat16),
            pltpu.VMEM((len(groups), units, count * depth), jnp.bfloat16),
            pltpu.VMEM((slots, units), jnp.bfloat16),
            pltpu.VMEM((slots, units), jnp.float32),
            pltpu.SemaphoreType.DMA((len(groups) + 1, 1 + count)),
        ],
        compiler_params=pltpu.CompilerParams(vmem_limit_bytes=VMEM),
        name="project",
    )(received, *blocks, hidden, slot_weight)


def finish_kernel(routes_ref, slot_ref, crossing_ref, gate_ref, up_ref, grad_gate_ref, grad_up_ref, out_ref):
    ranks = crossing_ref.shape[0]
    cap = crossing_ref.shape[1] // 2
    slots = ranks * cap
    topk, tokens = routes_ref.shape
    slot = slot_ref[...]
    grads = jnp.zeros((ranks, tokens), jnp.float32)
    for j in range(cap):
        grads = grads + jnp.where(slot == float(j), crossing_ref[:, j : j + 1], 0.0)
    served = served_experts(ranks, tokens)
    for k in range(topk):
        hit = routes_ref[k : k + 1, :] == served
        out_ref[k : k + 1, :] = jnp.sum(jnp.where(hit, grads, 0.0), axis=0, keepdims=True)
    row = lax.broadcasted_iota(jnp.int32, (slots, ranks), 0)
    owner = row // cap == lax.broadcasted_iota(jnp.int32, (slots, ranks), 1)
    spread = jnp.dot(
        jnp.where(owner, 1.0, 0.0).astype(jnp.bfloat16),
        crossing_ref[:, cap:].astype(jnp.bfloat16),
        preferred_element_type=jnp.float32,
    )
    mine = lax.broadcasted_iota(jnp.int32, (slots, cap), 0) % cap == lax.broadcasted_iota(
        jnp.int32, (slots, cap), 1
    )
    weight = jnp.sum(jnp.where(mine, spread, 0.0), axis=1, keepdims=True)
    grad_gate_ref[...] = (weight * gate_ref[...]).astype(jnp.bfloat16)
    grad_up_ref[...] = (weight * up_ref[...]).astype(jnp.bfloat16)


def finish(routes, slot, crossing, gate, up):
    out = jax.ShapeDtypeStruct(gate.shape, jnp.bfloat16)
    return pl.pallas_call(
        finish_kernel,
        out_shape=(out, out, jax.ShapeDtypeStruct((routes.shape[1], routes.shape[0]), jnp.float32)),
        compiler_params=pltpu.CompilerParams(vmem_limit_bytes=24 * 2**20),
        name="finish",
    )(routes.T, slot, crossing, gate, up)


def fetch(block, axis, partner):
    return lax.ppermute(block, axis, [(partner(i), i) for i in range(lax.axis_size(axis))])


def turn(expert):
    return 1 - 2 * ((expert // 2) % 2)


def fetch_next(block):
    n_dp, ranks = lax.axis_size("dp"), lax.axis_size("expert")
    pairs = [((a + turn(b)) % n_dp * ranks + b, a * ranks + b) for a in range(n_dp) for b in range(ranks)]
    return lax.ppermute(block, ("dp", "expert"), pairs)


def gather_weight(own):
    size = lax.axis_size("context")

    def after(block):
        return fetch(block, "context", lambda i: (i + 1) % size)

    def before(block):
        return fetch(block, "context", lambda i: (i - 1) % size)

    one = fetch_next(own)
    two = fetch_next(one)
    near = jnp.concatenate([own, one])
    near_after, near_before = after(near), before(near)
    far = jnp.concatenate([two, fetch_next(two)])
    far, near_after, near_before = lax.optimization_barrier((far, near_after, near_before))
    far_after, far_before = after(far), before(far)
    return [(near, far), (near_after, far_after), (after(near_after), before(far_before)), (near_before, far_before)]


def exchange(rows, ranks):
    blocks = rows.reshape(ranks, -1, rows.shape[1])
    return lax.all_to_all(blocks, "expert", split_axis=0, concat_axis=0, tiled=True).reshape(rows.shape)


def body(grad_out, routes, route_weight, saved_gate, saved_up, down_weight):
    ranks = lax.axis_size("expert")
    n_dp, n_context = lax.axis_size("dp"), lax.axis_size("context")
    cap, units = saved_gate.shape[4:]
    slots = ranks * cap

    sent, slot_weight, slot = head(routes, route_weight, grad_out, ranks, cap, n_dp, n_context)
    received = exchange(sent, ranks)
    groups = gather_weight(down_weight)

    gate = saved_gate.reshape(slots, units).astype(jnp.float32)
    up = saved_up.reshape(slots, units).astype(jnp.float32)
    sigma = jax.nn.sigmoid(gate)
    hidden = lax.optimization_barrier((gate * sigma * up).astype(jnp.bfloat16))
    back, crossing = project(received, groups, hidden, slot_weight)
    crossing = lax.all_to_all(crossing, "expert", split_axis=0, concat_axis=0, tiled=True)
    by_gate = back * up * sigma * (1.0 + gate * (1.0 - sigma))
    by_up = back * gate * sigma
    grad_gate, grad_up, grad_weight = finish(routes, slot, crossing, by_gate, by_up)
    return grad_gate.reshape(saved_gate.shape), grad_up.reshape(saved_up.shape), grad_weight.T


def solution(mesh):
    tokens = P(("dp", "expert", "context"), None)
    saved = P("dp", "expert", "context", None, None, None)
    return jax.shard_map(
        body,
        mesh=mesh,
        in_specs=(tokens, tokens, tokens, saved, saved, P("expert", None, ("dp", "context"))),
        out_specs=(saved, saved, tokens),
        check_vma=False,
    )
```
